512 devices in a mesh: feat: 8 (over x, core), vert: 64 (over y, z).
Axes of the slice: x: 4, y: 4, z: 16, core: 2. Of those that a mesh axis runs over, the one named last changes fastest.
Arguments:
- features: bfloat16 [512, 131072], P('feat', 'vert'), may hold values from -6 to 6
- tiles: bfloat16 [64, 56, 128, 128], P('vert'), may hold values from -0.375 to 0.375
- tile_rows: int32 [64, 56], P('vert'), may hold values from 0 to 15, as said below
- tile_cols: int32 [64, 56], P('vert'), may hold values from 0 to 1023, as said below
- tile_counts: int32 [64], P('vert'), may hold values from 1 to 56, as said below
- weight: bfloat16 [512, 512], replicated, may hold values from -0.25 to 0.25
- output_gradient: bfloat16 [512, 131072], P(None, ('vert', 'feat')), may hold values from -6 to 6
Outputs:
- activation: bfloat16 [512, 131072], P(None, ('vert', 'feat'))
- weight_gradient: float32 [512, 512], replicated
- feature_grad: bfloat16 [512, 131072], P('feat', 'vert')
The draws below stay inside these ranges and needn't reach their ends.
Inputs may be any that keep to these rules, and one draw needn't show every extreme that they name: `tile_rows`: slots at or beyond a block's count are unused; their tiles and indices are arbitrary. The block of a column tile, tile_cols // 16, equals the slot's own block or differs from it in exactly one of the lowest 4 bits. `tile_counts`: some block uses all 56 slots.
All inputs are finite; a program needn't handle non-finite values.
Results may differ from the reference program's by a relative error of at most 0.02.
Values may be sent and summed in bfloat16 or wider, within the bound.
A program may use at most 64 MiB of HBM per device.

```python
import jax
import jax.numpy as jnp
from jax import lax

F = 512
TILE = 128
LEVELS = 4
V_DEV = 2048
NB = 64
NV = 131072
RT = 16
CAP = 56


def draw_tile_rows(key, part):
    return jax.random.randint(jax.random.fold_in(key, 5), (NB, CAP), 0, RT).astype(jnp.int32)


def draw_tile_cols(key, part):
    level = jax.random.randint(jax.random.fold_in(key, 11), (NB, CAP), 0, LEVELS + 1).astype(jnp.int32)
    local = jax.random.randint(jax.random.fold_in(key, 12), (NB, CAP), 0, RT).astype(jnp.int32)
    level = level.at[0, 0].set(0).at[NB - 1, 0].set(0)
    local = local.at[0, 0].set(0).at[NB - 1, 0].set(RT - 1)
    home = jnp.arange(NB, dtype=jnp.int32)[:, None]
    flip = jnp.left_shift(jnp.int32(1), jnp.maximum(level - 1, 0)).astype(jnp.int32)
    block = jnp.where(level > 0, jnp.bitwise_xor(home, flip), home)
    return (block * RT + local).astype(jnp.int32)


def draw_tile_counts(key, part):
    base = jax.random.randint(jax.random.fold_in(key, 21), (NB,), CAP // 8 + 1, CAP + 1)
    fullest = jax.random.randint(jax.random.fold_in(key, 22), (), 0, NB)
    return jnp.where(jnp.arange(NB, dtype=jnp.int32) == fullest, CAP, base).astype(jnp.int32)


def shard_levels(own_key, shape, pieces, least, top_value):
    def one(dim, blocks):
        heights = jax.random.uniform(jax.random.fold_in(jax.random.fold_in(own_key, 6), dim), (blocks,), jnp.float32, least / len(pieces), top_value / len(pieces))
        return jnp.repeat(jnp.exp(heights), shape[dim] // blocks).reshape((-1,) + (1,) * (len(shape) - dim - 1))

    factor_of = one(*pieces[0])
    for cut in pieces[1:]:
        factor_of = factor_of * one(*cut)
    return factor_of


def noise(own_key, extent, width, most, split=(), kind=jnp.bfloat16):
    level = shard_levels(own_key, extent, split, -0.22, 0.18) if split else 1.0
    result = jax.random.normal(own_key, extent, jnp.float32) * width * level
    return jnp.minimum(jnp.maximum(result, -most), most).astype(kind)


def setup_inputs(seed: int = 0) -> dict:
    streams_of = jax.random.split(jax.random.key(seed), 8)
    features = noise(streams_of[0], (F, NV), 1.0, 6.0, ((0, 8), (1, 64)))
    tiles = noise(streams_of[1], (NB, CAP, TILE, TILE), (1.0 / (2 * TILE) ** 0.5), 0.375, ((0, 64),))
    tile_rows = draw_tile_rows(jax.random.fold_in(streams_of[7], 71), 0)
    tile_cols = draw_tile_cols(jax.random.fold_in(streams_of[7], 71), 0)
    tile_counts = draw_tile_counts(jax.random.fold_in(streams_of[7], 71), 0)
    weight = noise(streams_of[5], (F, F), F ** -0.5, 0.25)
    output_gradient = noise(streams_of[6], (F, NV), 1.0, 6.0, ((1, 512),))
    return {"features": features, "tiles": tiles, "tile_rows": tile_rows, "tile_cols": tile_cols, "tile_counts": tile_counts, "weight": weight, "output_gradient": output_gradient}


def reference(features, tiles, tile_rows, tile_cols, tile_counts, weight, output_gradient):
    row_tiles = V_DEV // TILE
    total_tiles = NB * row_tiles
    slots = jnp.arange(CAP, dtype=jnp.int32)
    feat_tiles = features.reshape(F, total_tiles, TILE)

    def forward_block(inputs):
        block_tiles, rows, cols, count = inputs
        valid = (slots < count).astype(jnp.float32)
        picked = feat_tiles[:, cols, :].astype(jnp.float32)
        share_value = jnp.einsum('fck,crk->cfr', picked, block_tiles.astype(jnp.float32))
        indicator_matrix = (rows[None, :] == jnp.arange(row_tiles, dtype=jnp.int32)[:, None]).astype(jnp.float32) * valid[None, :]
        reduced_total = jnp.einsum('zy,yqw->qzw', indicator_matrix, share_value)
        return reduced_total.reshape(F, V_DEV).astype(jnp.bfloat16)

    blocks = lax.map(forward_block, (tiles, tile_rows, tile_cols, tile_counts))
    aggregated = jnp.transpose(blocks, (1, 0, 2)).reshape(F, NV)
    pre = jnp.dot(weight.T, aggregated, preferred_element_type=jnp.float32)
    sigma = jax.nn.sigmoid(pre)
    activation = (pre * sigma).astype(jnp.bfloat16)
    pre_grad = (output_gradient.astype(jnp.float32) * sigma * (1.0 + pre * (1.0 - sigma))).astype(jnp.bfloat16)
    weight_gradient = jnp.dot(aggregated, pre_grad.T, preferred_element_type=jnp.float32)
    agg_grad = jnp.dot(weight, pre_grad, preferred_element_type=jnp.float32).astype(jnp.bfloat16)
    grad_tiles = agg_grad.reshape(F, total_tiles, TILE)
    bits = jnp.left_shift(jnp.int32(1), jnp.arange(LEVELS, dtype=jnp.int32)).astype(jnp.int32)
    targets = jnp.arange((LEVELS + 1) * row_tiles, dtype=jnp.int32)

    def backward_block(accum, inputs):
        block_tiles, rows, cols, count, index = inputs
        valid = (slots < count).astype(jnp.float32)
        local = lax.dynamic_slice_in_dim(grad_tiles, (index * row_tiles).astype(jnp.int32), row_tiles, 1)
        picked = local[:, rows, :].astype(jnp.float32)
        share_value = jnp.einsum('fcr,crk->cfk', picked, block_tiles.astype(jnp.float32)) * valid[:, None, None]
        differ = jnp.bitwise_xor(cols // row_tiles, index)
        level = jnp.zeros(cols.shape, jnp.int32)
        for bit in range(LEVELS):
            level = level + jnp.where(differ == (1 << bit), bit + 1, 0).astype(jnp.int32)
        slot_index = level * row_tiles + cols % row_tiles
        placing = (slot_index[None, :] == targets[:, None]).astype(jnp.float32)
        spread = jnp.einsum('sc,cfk->sfk', placing, share_value).reshape(LEVELS + 1, row_tiles, F, TILE)
        spread = jnp.transpose(spread, (0, 2, 1, 3)).reshape(LEVELS + 1, F, V_DEV)
        distant_block = lax.optimization_barrier(spread[1:].astype(jnp.bfloat16)).astype(jnp.float32)
        accum = accum.at[index].add(spread[0])
        dests = jnp.bitwise_xor(index, bits).astype(jnp.int32)
        accum = accum.at[dests].add(distant_block)
        return accum, None

    start = jnp.zeros((NB, F, V_DEV), jnp.float32)
    accum, unused = lax.scan(backward_block, start, (tiles, tile_rows, tile_cols, tile_counts, jnp.arange(NB, dtype=jnp.int32)))
    feature_grad = jnp.transpose(accum, (1, 0, 2)).reshape(F, NV).astype(jnp.bfloat16)
    return activation, weight_gradient, feature_grad
```

```python
import functools

import jax
import jax.numpy as jnp
from jax import lax
from jax.experimental import pallas as pl
from jax.experimental.pallas import tpu as pltpu
from jax.sharding import PartitionSpec as P

NZ = 16
LEVELS = 4
CHUNKS = 4
GROUP = 8
MESH = pl.DeviceIdType.MESH
BF16, F32 = jnp.bfloat16, jnp.float32
NT = (((1,), (1,)), ((), ()))


def offsets(slots, row_tiles):
    sizes = (slots, slots, slots, slots, row_tiles, (LEVELS + 1) * row_tiles)
    starts = [0]
    for size in sizes:
        starts.append(starts[-1] + size)
    return starts


def index_kernel(slots, row_tiles, rows_ref, cols_ref, count_ref, out_ref):
    src, row, prev_f, prev_b, last_f, last_b, end = offsets(slots, row_tiles)
    block = lax.axis_index("vert")
    count = count_ref[0]

    def clear(i, carry):
        out_ref[last_f + i] = jnp.int32(slots)
        return carry

    lax.fori_loop(0, end - last_f, clear, 0)

    def step(c, carry):
        valid = c < count
        col = cols_ref[0, c]
        differ = (col // row_tiles) ^ block
        level = jnp.int32(0)
        for bit in range(LEVELS):
            level = level + jnp.where(differ >= (1 << bit), 1, 0).astype(jnp.int32)
        tile = jnp.where(valid, level * row_tiles + col % row_tiles, 0)
        line = jnp.where(valid, rows_ref[0, c], 0)
        out_ref[src + c] = tile
        out_ref[row + c] = line
        before = out_ref[last_f + line]
        out_ref[prev_f + c] = before
        out_ref[last_f + line] = jnp.where(valid, c, before)
        before = out_ref[last_b + tile]
        out_ref[prev_b + c] = before
        out_ref[last_b + tile] = jnp.where(valid, c, before)
        return carry

    lax.fori_loop(0, slots, step, 0)


def layer_kernel(
    nf, ny, slots, row_tiles, tile,
    idx, feat, tiles, weight, out_grad,
    act, wgrad, fgrad,
    stk, acc, wt, agg, full, pg, ag, gc, wgs, frs, red, yr, zs, zr, zsum, zh, zag, yag,
    part, rly, mrg, rv, ssem, rsem,
):
    src, row, prev_f, prev_b, last_f, last_b, _ = offsets(slots, row_tiles)
    fl = feat.shape[0]
    f_all = nf * fl
    per = row_tiles // nf
    me_f, me_v = lax.axis_index("feat"), lax.axis_index("vert")
    z, y = me_v % NZ, me_v // NZ
    zl, zhi = z % 4, z // 4
    piece = row_tiles // CHUNKS

    used = [0]

    def send(source, dest, f, v):
        n = used[0]
        used[0] += 1
        copy = pltpu.make_async_remote_copy(
            source, dest, ssem.at[n], rsem.at[n], device_id=(f, v), device_id_type=MESH
        )
        copy.start()
        return copy

    peers = [(me_f ^ d, me_v) for d in range(1, nf)]
    peers += [(me_f, me_v ^ d) for d in (1, 2, 3, 4, 8, 12)]
    peers += [(me_f, (y ^ d) * NZ + z) for d in range(1, ny)]
    barrier = pltpu.get_barrier_semaphore()
    for f, v in peers:
        pl.semaphore_signal(barrier, inc=1, device_id=(f, v), device_id_type=MESH)
    for t in range(row_tiles):
        stk[t] = feat[:, t * tile : (t + 1) * tile]
    pl.semaphore_wait(barrier, len(peers))

    def rows_of(level, k):
        return pl.ds(level * row_tiles + k * piece, piece)

    waits = []
    first = [
        send(stk.at[rows_of(0, k)], stk.at[rows_of(3, k)], me_f, me_v ^ 4) for k in range(CHUNKS)
    ]
    for bit in (1, 0):
        waits.append(
            send(
                stk.at[pl.ds(0, row_tiles)],
                stk.at[pl.ds((bit + 1) * row_tiles, row_tiles)],
                me_f,
                me_v ^ (1 << bit),
            )
        )
    acc[slots] = jnp.zeros(acc.shape[1:], F32)
    wt[...] = weight[...].astype(F32).T.astype(BF16)
    for k, copy in enumerate(first):
        copy.wait()
        waits.append(send(stk.at[rows_of(3, k)], stk.at[rows_of(4, k)], me_f, me_v ^ 12))
    for copy in waits:
        copy.wait()

    def forward(g, carry):
        products = []
        for u in range(GROUP):
            c = g * GROUP + u
            picked = stk[idx[src + c]]
            products.append(
                lax.dot_general(picked, tiles[c], NT, preferred_element_type=F32)
            )
        for u in range(GROUP):
            c = g * GROUP + u
            acc[c] = products[u] + acc[idx[prev_f + c]]
        return carry

    lax.fori_loop(0, slots // GROUP, forward, 0)

    for r in range(row_tiles):
        k = r % per
        agg[r // per, :, k * tile : (k + 1) * tile] = acc[idx[last_f + r]].astype(BF16)
    full[me_f] = agg[me_f]
    waits = []
    for d in range(1, nf):
        waits.append(send(agg.at[me_f ^ d], full.at[me_f], me_f ^ d, me_v))
    for copy in waits:
        copy.wait()

    share = per * tile
    rows = full[...].reshape(f_all, share)
    halves = 2
    h = f_all // halves
    for i in range(halves):
        part_rows = slice(i * h, (i + 1) * h)
        pre = jnp.dot(wt[part_rows, :], rows, preferred_element_type=F32)
        sigma = jax.nn.sigmoid(pre)
        act[part_rows, :] = (pre * sigma).astype(BF16)
        pg[part_rows, :] = (
            out_grad[part_rows, :].astype(F32) * sigma * (1.0 + pre * (1.0 - sigma))
        ).astype(BF16)
    grads = pg[...]
    for i in range(halves):
        part_rows = slice(i * h, (i + 1) * h)
        agg_grad = jnp.dot(weight[part_rows, :], grads, preferred_element_type=F32).astype(BF16)
        for k in range(per):
            ag[i * nf // halves : (i + 1) * nf // halves, k] = agg_grad[
                :, k * tile : (k + 1) * tile
            ].reshape(nf // halves, fl, tile)
    back = []
    mine = pl.ds(me_f * per, per)
    for d in range(1, nf):
        back.append(send(ag.at[me_f ^ d], gc.at[mine], me_f ^ d, me_v))
    gc[mine] = ag[me_f]
    for j in range(nf):
        wgs[j] = lax.dot_general(full[j], pg[...], NT, preferred_element_type=F32).astype(BF16)
    terms = [send(wgs.at[me_f ^ d], frs.at[me_f], me_f ^ d, me_v) for d in range(1, nf)]
    frs[me_f] = wgs[me_f]
    for copy in back:
        copy.wait()

    def backward(g, carry):
        products = []
        for u in range(GROUP):
            c = g * GROUP + u
            picked = gc[idx[row + c]]
            products.append(jnp.dot(picked, tiles[c], preferred_element_type=F32))
        for u in range(GROUP):
            c = g * GROUP + u
            acc[c] = products[u] + acc[idx[prev_b + c]]
        return carry

    lax.fori_loop(0, slots // GROUP, backward, 0)

    def summed(level, t):
        return acc[idx[last_b + level * row_tiles + t]]

    waits, relayed = [], []
    for k in range(CHUNKS):
        for t in range(k * piece, (k + 1) * piece):
            part[2, t] = summed(4, t).astype(BF16)
        span = pl.ds(k * piece, piece)
        relayed.append(send(part.at[2, span], rly.at[span], me_f, me_v ^ 12))
    for bit in (1, 0):
        for t in range(row_tiles):
            part[bit, t] = summed(bit + 1, t).astype(BF16)
        waits.append(send(part.at[bit], rv.at[bit], me_f, me_v ^ (1 << bit)))

    merged = []

    def relay(k):
        relayed[k].wait()
        for t in range(k * piece, (k + 1) * piece):
            mrg[t] = (summed(3, t) + rly[t].astype(F32)).astype(BF16)
        span = pl.ds(k * piece, piece)
        merged.append(send(mrg.at[span], rv.at[2, span], me_f, me_v ^ 4))

    for copy in terms:
        copy.wait()
    total = frs[0].astype(F32)
    for j in range(1, nf):
        total = total + frs[j].astype(F32)
    slab = fl // ny
    red[...] = total.reshape(ny, slab, f_all)
    yr[y] = red[y]
    step = [send(red.at[y ^ d], yr.at[y], me_f, (y ^ d) * NZ + z) for d in range(1, ny)]
    relay(0)
    for copy in step:
        copy.wait()
    total = yr[0]
    for j in range(1, ny):
        total = total + yr[j]
    hr, hc = slab // 2, f_all // 2
    for q in range(4):
        zs[q] = total[q // 2 * hr : (q // 2 + 1) * hr, q % 2 * hc : (q % 2 + 1) * hc]
    zr[zl] = zs[zl]
    step = [send(zs.at[zl ^ d], zr.at[zl], me_f, me_v ^ d) for d in range(1, 4)]
    relay(1)
    for copy in step:
        copy.wait()
    zsum[...] = zr[0] + zr[1] + zr[2] + zr[3]
    zh[zhi] = zsum[...]
    step = [send(zsum, zh.at[zhi], me_f, me_v ^ (4 * d)) for d in range(1, 4)]
    relay(2)
    for copy in step:
        copy.wait()
    zag[zl] = zh[0] + zh[1] + zh[2] + zh[3]
    step = [send(zag.at[zl], zag.at[zl], me_f, me_v ^ d) for d in range(1, 4)]
    relay(3)
    for copy in step:
        copy.wait()
    for q in range(4):
        yag[y, q // 2 * hr : (q // 2 + 1) * hr, q % 2 * hc : (q % 2 + 1) * hc] = zag[q]
    step = [send(yag.at[y], yag.at[y], me_f, (y ^ d) * NZ + z) for d in range(1, ny)]
    for copy in step:
        copy.wait()
    wgrad[me_f] = yag[...].reshape(fl, f_all)
    step = [
        send(wgrad.at[me_f], wgrad.at[me_f], me_f ^ (2 * d), me_v) for d in range(1, nf // 2)
    ]
    last = [send(wgrad.at[me_f], wgrad.at[me_f], me_f ^ 1, me_v)]
    for d, copy in enumerate(step, 1):
        copy.wait()
        other = me_f ^ (2 * d)
        last.append(send(wgrad.at[other], wgrad.at[other], me_f ^ 1, me_v))
    for copy in waits:
        copy.wait()
    for k in range(CHUNKS):
        merged[k].wait()
        for t in range(k * piece, (k + 1) * piece):
            sums = summed(0, t) + rv[0, t].astype(F32) + rv[1, t].astype(F32)
            fgrad[:, t * tile : (t + 1) * tile] = (sums + rv[2, t].astype(F32)).astype(BF16)
    for copy in last:
        copy.wait()


def body(features, tiles, tile_rows, tile_cols, tile_counts, weight, output_gradient):
    fl, vdev = features.shape
    slots, tile = tiles.shape[1], tiles.shape[2]
    row_tiles = vdev // tile
    nf, nv = lax.axis_size("feat"), lax.axis_size("vert")
    ny = nv // NZ
    f_all, share = output_gradient.shape
    smem = pl.BlockSpec(memory_space=pltpu.SMEM)
    vmem = pl.BlockSpec(memory_space=pltpu.VMEM)
    index = pl.pallas_call(
        functools.partial(index_kernel, slots, row_tiles),
        out_shape=jax.ShapeDtypeStruct((offsets(slots, row_tiles)[-1],), jnp.int32),
        in_specs=[smem] * 3,
        out_specs=smem,
    )(tile_rows, tile_cols, tile_counts)
    slab = fl // ny
    copies = 2 * (2 + 2 * CHUNKS) + 3 * (nf - 1) + 2 * (ny - 1) + 9 + (nf // 2 - 1) + nf // 2
    scratch = [
        ((LEVELS + 1) * row_tiles, fl, tile, BF16),
        (slots + 1, fl, tile, F32),
        (f_all, f_all, BF16),
        (nf, fl, share, BF16),
        (nf, fl, share, BF16),
        (f_all, share, BF16),
        (nf, row_tiles // nf, fl, tile, BF16),
        (row_tiles, fl, tile, BF16),
        (nf, fl, f_all, BF16),
        (nf, fl, f_all, BF16),
        (ny, slab, f_all, F32),
        (ny, slab, f_all, F32),
        (4, slab // 2, f_all // 2, F32),
        (4, slab // 2, f_all // 2, F32),
        (slab // 2, f_all // 2, F32),
        (4, slab // 2, f_all // 2, F32),
        (4, slab // 2, f_all // 2, F32),
        (ny, slab, f_all, F32),
        (3, row_tiles, fl, tile, BF16),
        (row_tiles, fl, tile, BF16),
        (row_tiles, fl, tile, BF16),
        (3, row_tiles, fl, tile, BF16),
    ]
    act, wgrad, fgrad = pl.pallas_call(
        functools.partial(layer_kernel, nf, ny, slots, row_tiles, tile),
        out_shape=(
            jax.ShapeDtypeStruct((f_all, share), BF16),
            jax.ShapeDtypeStruct((nf, fl, f_all), F32),
            jax.ShapeDtypeStruct((fl, vdev), BF16),
        ),
        in_specs=[smem] + [vmem] * 4,
        out_specs=(vmem, vmem, vmem),
        scratch_shapes=[pltpu.VMEM(s[:-1], s[-1]) for s in scratch]
        + [pltpu.SemaphoreType.DMA((copies,)), pltpu.SemaphoreType.DMA((copies,))],
        compiler_params=pltpu.CompilerParams(
            collective_id=0, has_side_effects=True, vmem_limit_bytes=40 * 1024 * 1024
        ),
    )(index, features, tiles[0], weight, output_gradient)
    return act, wgrad.reshape(f_all, f_all), fgrad


def solution(mesh):
    in_specs = (
        P("feat", "vert"),
        P("vert", None, None, None),
        P("vert", None),
        P("vert", None),
        P("vert"),
        P(),
        P(None, ("vert", "feat")),
    )
    out_specs = (P(None, ("vert", "feat")), P(), P("feat", "vert"))
    return jax.shard_map(body, mesh=mesh, in_specs=in_specs, out_specs=out_specs, check_vma=False)
```

```python
import functools

import jax
import jax.numpy as jnp
from jax import lax
from jax.experimental import pallas as pl
from jax.experimental.pallas import tpu as pltpu
from jax.sharding import PartitionSpec as P

NZ = 16
LEVELS = 4
HALVES = 2
CHUNKS = 4
ORDER = (
    ("products", 0),
    ("near", 0),
    ("products", 1),
    ("scatter",),
    ("far", 0),
    ("near", 1),
    ("relay", 1),
    ("gather",),
    ("far", 1),
    ("relay", 2),
    ("spread",),
    ("relay", 1),
    ("pass",),
)
BACK = 2
GROUP = 8
SRC, ROW, PREV_F, PREV_B, LAST_F, LAST_B = range(6)
LANES = 128
MESH = pl.DeviceIdType.MESH
BF16, F32, I32 = jnp.bfloat16, jnp.float32, jnp.int32
NT = (((1,), (1,)), ((), ()))


def index_table(slots, row_tiles, rows, cols, count, table):
    across = lax.broadcasted_iota(I32, (slots, slots), 1)
    down = lax.broadcasted_iota(I32, (slots, slots), 0)
    wide = lax.broadcasted_iota(I32, (slots, LANES), 1)
    deep = lax.broadcasted_iota(I32, (slots, LANES), 0)
    valid = lax.broadcasted_iota(I32, (1, slots), 1) < count
    shift = row_tiles.bit_length() - 1
    differ = lax.shift_right_arithmetic(cols, shift) ^ lax.axis_index("vert")
    level = jnp.zeros(cols.shape, I32)
    for bit in range(LEVELS):
        level = level + jnp.where(differ >= (1 << bit), 1, 0).astype(I32)
    target = jnp.where(valid, level * row_tiles + (cols & (row_tiles - 1)), 0)
    line = jnp.where(valid, rows, 0)
    table[SRC : SRC + 1, :slots] = target
    table[ROW : ROW + 1, :slots] = line
    for key, prev_at, last_at in ((line, PREV_F, LAST_F), (target, PREV_B, LAST_B)):
        key = jnp.where(valid, key, -1)
        column = jnp.max(jnp.where(across == down, key, -1), axis=1, keepdims=True)
        same = (column == key) & (down < across) & (column >= 0)
        before = jnp.max(jnp.where(same, down, -1), axis=0, keepdims=True)
        table[prev_at : prev_at + 1, :slots] = jnp.where(before < 0, slots, before)
        final = jnp.max(jnp.where(column == wide, deep, -1), axis=0, keepdims=True)
        table[last_at : last_at + 1, :] = jnp.where(final < 0, slots, final)


def layer_kernel(
    nf, ny, slots, row_tiles, tile,
    counts, rows_in, cols_in, feat_in, tiles_in, weight_in, grad_in,
    act, wgrad, fgrad,
    table, feat, tiles, weight, out_grad,
    stk0, stk1, acc, wt, agg, full, pg, ag, gc0, gc1, wgs, frs, zs, zr, zag, total_of, pag,
    part, rly, mrg, rv, idx, lsem, ssem, rsem,
):
    stk, gc = (stk0, stk1), (gc0, gc1)
    fl = feat.shape[0]
    f_all = nf * fl
    hl = fl // HALVES
    per = row_tiles // nf
    share = per * tile
    me_f, me_v = lax.axis_index("feat"), lax.axis_index("vert")
    z, y = me_v % NZ, me_v // NZ
    piece, bpiece = row_tiles // CHUNKS, row_tiles // BACK

    used = [0]

    def send(source, dest, f, v):
        n = used[0]
        used[0] += 1
        copy = pltpu.make_async_remote_copy(
            source, dest, ssem.at[n], rsem.at[n], device_id=(f, v), device_id_type=MESH
        )
        copy.start()
        return copy

    def fetch(source, dest, n):
        copy = pltpu.make_async_copy(source, dest, lsem.at[n])
        copy.start()
        return copy

    peers = [(me_f, me_v ^ d) for d in range(NZ - 1, 0, -1)]
    plane = [(df, dy) for df in range(nf) for dy in range(ny) if df or dy]
    peers += [(me_f ^ df, (y ^ dy) * NZ + z) for df, dy in plane]
    barrier = pltpu.get_barrier_semaphore()
    for f, v in peers:
        pl.semaphore_signal(barrier, inc=1, device_id=(f, v), device_id_type=MESH)
    get_feat = fetch(feat_in, feat, 0)
    get_weight = fetch(weight_in, weight, 1)
    get_tiles = fetch(tiles_in, tiles, 2)
    get_grad = fetch(grad_in, out_grad, 3)
    get_feat.wait()
    for hf in range(HALVES):
        for t in range(row_tiles):
            stk[hf][t] = feat[hf * hl : (hf + 1) * hl, t * tile : (t + 1) * tile]
    pl.semaphore_wait(barrier, len(peers))

    def span_of(level, k):
        return pl.ds(level * row_tiles + k * piece, piece)

    def start_features(hf):
        first = [
            send(stk[hf].at[span_of(0, k)], stk[hf].at[span_of(3, k)], me_f, me_v ^ 4)
            for k in range(CHUNKS)
        ]
        direct = [
            send(
                stk[hf].at[pl.ds(0, row_tiles)],
                stk[hf].at[pl.ds((bit + 1) * row_tiles, row_tiles)],
                me_f,
                me_v ^ (1 << bit),
            )
            for bit in (1, 0)
        ]
        return first, direct

    def hand_on(hf, first):
        handed = []
        for k, copy in enumerate(first):
            copy.wait()
            handed.append(send(stk[hf].at[span_of(3, k)], stk[hf].at[span_of(4, k)], me_f, me_v ^ 12))
        return handed

    def chain(out, picked, use_nt, prev):
        def some(g, carry):
            products = []
            for u in range(GROUP):
                c = g * GROUP + u
                if use_nt:
                    products.append(
                        lax.dot_general(picked(c), tiles[0, c], NT, preferred_element_type=F32)
                    )
                else:
                    products.append(jnp.dot(picked(c), tiles[0, c], preferred_element_type=F32))
            for u in range(GROUP):
                c = g * GROUP + u
                out[c] = products[u] + out[idx[prev, c]]
            return carry

        lax.fori_loop(0, slots // GROUP, some, 0)

    def aggregate(hf):
        chain(acc.at[hf], lambda c: stk[hf][idx[SRC, c]], True, PREV_F)
        for r in range(row_tiles):
            k = r % per
            agg[hf, r // per, :, k * tile : (k + 1) * tile] = acc[hf, idx[LAST_F, r]].astype(BF16)
        full[hf, me_f] = agg[hf, me_f]
        return [
            send(agg.at[hf, me_f ^ d], full.at[hf, me_f], me_f ^ d, me_v) for d in range(1, nf)
        ]

    first, direct = start_features(0)
    index_table(slots, row_tiles, rows_in[...], cols_in[...], counts[0], table)
    get_index = fetch(table, idx, 4)
    for hf in range(HALVES):
        acc[hf, slots] = jnp.zeros(acc.shape[2:], F32)
    get_weight.wait()
    for hf in range(HALVES):
        mine = weight[...].reshape(nf, HALVES, hl, f_all)[:, hf].reshape(f_all // HALVES, f_all)
        wt[hf] = mine.astype(F32).T.astype(BF16)
    get_index.wait()
    get_tiles.wait()
    get_grad.wait()
    moves = []
    for hf in range(HALVES):
        handed = hand_on(hf, first)
        arrivals = direct + handed
        if hf + 1 < HALVES:
            first, direct = start_features(hf + 1)
        for copy in arrivals:
            copy.wait()
        moves.append(aggregate(hf))

    blocks = 2
    block = f_all // blocks
    for hf in range(HALVES):
        for copy in moves[hf]:
            copy.wait()
    rows = [full[hf].reshape(f_all // HALVES, share) for hf in range(HALVES)]
    for i in range(blocks):
        at = slice(i * block, (i + 1) * block)
        pre = jnp.dot(wt[0, at, :], rows[0], preferred_element_type=F32)
        for hf in range(1, HALVES):
            pre = pre + jnp.dot(wt[hf, at, :], rows[hf], preferred_element_type=F32)
        sigma = jax.nn.sigmoid(pre)
        act[at, :] = (pre * sigma).astype(BF16)
        pg[at, :] = (
            out_grad[at, :].astype(F32) * sigma * (1.0 + pre * (1.0 - sigma))
        ).astype(BF16)
    grads = pg[...]
    mine = pl.ds(me_f * per, per)
    back = []
    for hf in range(HALVES):
        own = weight[...].reshape(nf, HALVES, hl, f_all)[:, hf].reshape(f_all // HALVES, f_all)
        agg_grad = jnp.dot(own, grads, preferred_element_type=F32).astype(BF16)
        for k in range(per):
            ag[hf, :, k] = agg_grad[:, k * tile : (k + 1) * tile].reshape(nf, hl, tile)
        back.append(
            [send(ag.at[hf, me_f ^ d], gc[hf].at[mine], me_f ^ d, me_v) for d in range(1, nf)]
        )
        gc[hf][mine] = ag[hf, me_f]
    for hf in range(HALVES):
        term = lax.dot_general(rows[hf], grads, NT, preferred_element_type=F32).astype(BF16)
        wgs[:, hf * hl : (hf + 1) * hl, :] = term.reshape(nf, hl, f_all)
    slab = fl // ny
    me_p = me_f * ny + y
    terms = [
        send(
            wgs.at[me_f ^ df, pl.ds((y ^ dy) * slab, slab)],
            frs.at[me_p],
            me_f ^ df,
            (y ^ dy) * NZ + z,
        )
        for df, dy in plane
    ]
    frs[me_p] = wgs[me_f, pl.ds(y * slab, slab)]

    def summed(hf, level, t):
        return acc[hf, idx[LAST_B, level * row_tiles + t]]

    direct, relayed, merged, last, steps = [], [], [], [], {}
    hr, hc = slab // 4, f_all // 4
    parts = [
        (slice(q // 4 * hr, (q // 4 + 1) * hr), slice(q % 4 * hc, (q % 4 + 1) * hc))
        for q in range(NZ)
    ]
    same_core = [(df, dy) for df, dy in plane if df % 2 == 0]

    def products(hf):
        for copy in back[hf]:
            copy.wait()
        chain(acc.at[hf], lambda c: gc[hf][idx[ROW, c]], False, PREV_B)

    def far(hf):
        for k in range(BACK):
            for t in range(k * bpiece, (k + 1) * bpiece):
                part[hf, 2, t] = summed(hf, 4, t).astype(BF16)
            span = pl.ds(k * bpiece, bpiece)
            relayed.append(send(part.at[hf, 2, span], rly.at[hf, span], me_f, me_v ^ 12))

    def near(hf):
        for bit in (1, 0):
            for t in range(row_tiles):
                part[hf, bit, t] = summed(hf, bit + 1, t).astype(BF16)
            direct.append(send(part.at[hf, bit], rv.at[hf, bit], me_f, me_v ^ (1 << bit)))

    def relay(count):
        for n in range(len(merged), len(merged) + count):
            hf, k = divmod(n, BACK)
            relayed[n].wait()
            for t in range(k * bpiece, (k + 1) * bpiece):
                mrg[hf, t] = (summed(hf, 3, t) + rly[hf, t].astype(F32)).astype(BF16)
            span = pl.ds(k * bpiece, bpiece)
            merged.append(send(mrg.at[hf, span], rv.at[hf, 2, span], me_f, me_v ^ 4))

    def scatter():
        for copy in terms:
            copy.wait()
        total = frs[0].astype(F32)
        for p in range(1, nf * ny):
            total = total + frs[p].astype(F32)
        for q, (at_r, at_c) in enumerate(parts):
            zs[q] = total[at_r, at_c]
        zr[z] = zs[z]
        steps["z"] = [send(zs.at[z ^ d], zr.at[z], me_f, me_v ^ d) for d in range(NZ - 1, 0, -1)]

    def gather():
        for copy in steps["z"]:
            copy.wait()
        total = zr[0]
        for q in range(1, NZ):
            total = total + zr[q]
        zag[z] = total
        steps["z"] = [send(zag.at[z], zag.at[z], me_f, me_v ^ d) for d in range(NZ - 1, 0, -1)]

    def spread():
        for copy in steps["z"]:
            copy.wait()
        for q, (at_r, at_c) in enumerate(parts):
            total_of[at_r, at_c] = zag[q]
        pag[me_p] = total_of[...].astype(BF16)
        steps["p"] = [
            send(pag.at[me_p], pag.at[me_p], me_f ^ df, (y ^ dy) * NZ + z) for df, dy in same_core
        ]
        last.append(send(pag.at[me_p], pag.at[me_p], me_f ^ 1, me_v))

    def pass_over():
        for (df, dy), copy in zip(same_core, steps["p"]):
            copy.wait()
            other = (me_f ^ df) * ny + (y ^ dy)
            last.append(send(pag.at[other], pag.at[other], me_f ^ 1, me_v))

    for name, *args in ORDER:
        {
            "products": products, "far": far, "near": near, "relay": relay, "scatter": scatter,
            "gather": gather, "spread": spread, "pass": pass_over,
        }[name](*args)
    for copy in direct + merged:
        copy.wait()
    for hf in range(HALVES):
        for t in range(row_tiles):
            sums = summed(hf, 0, t)
            for bit in range(3):
                sums = sums + rv[hf, bit, t].astype(F32)
            fgrad[hf * hl : (hf + 1) * hl, t * tile : (t + 1) * tile] = sums.astype(BF16)
    for copy in last:
        copy.wait()
    for f in range(nf):
        wgrad[f] = pag[f * ny : (f + 1) * ny].reshape(fl, f_all).astype(F32)


def body(features, tiles, tile_rows, tile_cols, tile_counts, weight, output_gradient):
    fl, vdev = features.shape
    slots, tile = tiles.shape[1], tiles.shape[2]
    row_tiles = vdev // tile
    nf, nv = lax.axis_size("feat"), lax.axis_size("vert")
    ny = nv // NZ
    f_all, share = output_gradient.shape
    smem = pl.BlockSpec(memory_space=pltpu.SMEM)
    vmem = pl.BlockSpec(memory_space=pltpu.VMEM)
    hbm = pl.BlockSpec(memory_space=pltpu.HBM)
    slab = fl // ny
    hl = fl // HALVES
    copies = HALVES * (4 + 2 * CHUNKS + 2 * BACK + 2 * (nf - 1))
    copies += (nf * ny - 1) + 2 * (NZ - 1) + (nf // 2 * ny - 1) + nf // 2 * ny
    scratch = [
        (8, LANES, I32),
        (fl, vdev, BF16),
        (1, slots, tile, tile, BF16),
        (f_all, f_all, BF16),
        (f_all, share, BF16),
        ((LEVELS + 1) * row_tiles, hl, tile, BF16),
        ((LEVELS + 1) * row_tiles, hl, tile, BF16),
        (HALVES, slots + 1, hl, tile, F32),
        (HALVES, f_all, f_all // HALVES, BF16),
        (HALVES, nf, hl, share, BF16),
        (HALVES, nf, hl, share, BF16),
        (f_all, share, BF16),
        (HALVES, nf, row_tiles // nf, hl, tile, BF16),
        (row_tiles, hl, tile, BF16),
        (row_tiles, hl, tile, BF16),
        (nf, fl, f_all, BF16),
        (nf * ny, slab, f_all, BF16),
        (NZ, slab // 4, f_all // 4, F32),
        (NZ, slab // 4, f_all // 4, F32),
        (NZ, slab // 4, f_all // 4, F32),
        (slab, f_all, F32),
        (nf * ny, slab, f_all, BF16),
        (HALVES, 3, row_tiles, hl, tile, BF16),
        (HALVES, row_tiles, hl, tile, BF16),
        (HALVES, row_tiles, hl, tile, BF16),
        (HALVES, 3, row_tiles, hl, tile, BF16),
    ]
    act, wgrad, fgrad = pl.pallas_call(
        functools.partial(layer_kernel, nf, ny, slots, row_tiles, tile),
        out_shape=(
            jax.ShapeDtypeStruct((f_all, share), BF16),
            jax.ShapeDtypeStruct((nf, fl, f_all), F32),
            jax.ShapeDtypeStruct((fl, vdev), BF16),
        ),
        in_specs=[smem, vmem, vmem] + [hbm] * 4,
        out_specs=(vmem, vmem, vmem),
        scratch_shapes=[pltpu.VMEM(s[:-1], s[-1]) for s in scratch]
        + [
            pltpu.SMEM((8, LANES), I32),
            pltpu.SemaphoreType.DMA((5,)),
            pltpu.SemaphoreType.DMA((copies,)),
            pltpu.SemaphoreType.DMA((copies,)),
        ],
        compiler_params=pltpu.CompilerParams(
            collective_id=0, has_side_effects=True, vmem_limit_bytes=58 * 1024 * 1024
        ),
    )(tile_counts, tile_rows, tile_cols, features, tiles, weight, output_gradient)
    return act, wgrad.reshape(f_all, f_all), fgrad


def solution(mesh):
    in_specs = (
        P("feat", "vert"),
        P("vert", None, None, None),
        P("vert", None),
        P("vert", None),
        P("vert"),
        P(),
        P(None, ("vert", "feat")),
    )
    out_specs = (P(None, ("vert", "feat")), P(), P("feat", "vert"))
    return jax.shard_map(body, mesh=mesh, in_specs=in_specs, out_specs=out_specs, check_vma=False)
```

```python
import functools

import jax
import jax.numpy as jnp
from jax import lax
from jax.experimental import pallas as pl
from jax.experimental.pallas import tpu as pltpu
from jax.sharding import PartitionSpec as P

NZ = 16
LEVELS = 4
HALVES = 2
CHUNKS = 4
ORDER = (
    ("products", 0),
    ("near", 0),
    ("products", 1),
    ("scatter",),
    ("far", 0),
    ("near", 1),
    ("relay", 2),
    ("gather",),
    ("far", 1),
    ("relay", 4),
    ("spread",),
    ("relay", 2),
    ("pass",),
)
BACK = 4
GROUP = 8
SRC, ROW, PREV_F, PREV_B, LAST_F, LAST_B = range(6)
LANES = 128
MESH = pl.DeviceIdType.MESH
BF16, F32, I32 = jnp.bfloat16, jnp.float32, jnp.int32
NT = (((1,), (1,)), ((), ()))


def index_table(slots, row_tiles, rows, cols, count, table):
    across = lax.broadcasted_iota(I32, (slots, slots), 1)
    down = lax.broadcasted_iota(I32, (slots, slots), 0)
    wide = lax.broadcasted_iota(I32, (slots, LANES), 1)
    deep = lax.broadcasted_iota(I32, (slots, LANES), 0)
    valid = lax.broadcasted_iota(I32, (1, slots), 1) < count
    shift = row_tiles.bit_length() - 1
    differ = lax.shift_right_arithmetic(cols, shift) ^ lax.axis_index("vert")
    level = jnp.zeros(cols.shape, I32)
    for bit in range(LEVELS):
        level = level + jnp.where(differ >= (1 << bit), 1, 0).astype(I32)
    target = jnp.where(valid, level * row_tiles + (cols & (row_tiles - 1)), 0)
    line = jnp.where(valid, rows, 0)
    table[SRC : SRC + 1, :slots] = target
    table[ROW : ROW + 1, :slots] = line
    for key, prev_at, last_at in ((line, PREV_F, LAST_F), (target, PREV_B, LAST_B)):
        key = jnp.where(valid, key, -1)
        column = jnp.max(jnp.where(across == down, key, -1), axis=1, keepdims=True)
        same = (column == key) & (down < across) & (column >= 0)
        before = jnp.max(jnp.where(same, down, -1), axis=0, keepdims=True)
        table[prev_at : prev_at + 1, :slots] = jnp.where(before < 0, slots, before)
        final = jnp.max(jnp.where(column == wide, deep, -1), axis=0, keepdims=True)
        table[last_at : last_at + 1, :] = jnp.where(final < 0, slots, final)


def layer_kernel(
    nf, ny, slots, row_tiles, tile,
    counts, rows_in, cols_in, feat_in, tiles_in, weight_in, grad_in,
    act, wgrad, fgrad,
    table, feat, tiles, weight, out_grad,
    stk0, stk1, acc, wt, agg, full, pg, ag, gc0, gc1, wgs, frs, zs, zr, zag, total_of, pag,
    part, rly, mrg, rv, idx, lsem, ssem, rsem,
):
    stk, gc = (stk0, stk1), (gc0, gc1)
    fl = feat.shape[0]
    f_all = nf * fl
    hl = fl // HALVES
    per = row_tiles // nf
    share = per * tile
    me_f, me_v = lax.axis_index("feat"), lax.axis_index("vert")
    z, y = me_v % NZ, me_v // NZ
    piece, bpiece = row_tiles // CHUNKS, row_tiles // BACK

    used = [0]

    def send(source, dest, f, v):
        n = used[0]
        used[0] += 1
        copy = pltpu.make_async_remote_copy(
            source, dest, ssem.at[n], rsem.at[n], device_id=(f, v), device_id_type=MESH
        )
        copy.start()
        return copy

    def fetch(source, dest, n):
        copy = pltpu.make_async_copy(source, dest, lsem.at[n])
        copy.start()
        return copy

    peers = [(me_f, me_v ^ d) for d in range(NZ - 1, 0, -1)]
    plane = [(df, dy) for df in range(nf) for dy in range(ny) if df or dy]
    peers += [(me_f ^ df, (y ^ dy) * NZ + z) for df, dy in plane]
    barrier = pltpu.get_barrier_semaphore()
    for f, v in peers:
        pl.semaphore_signal(barrier, inc=1, device_id=(f, v), device_id_type=MESH)
    get_feat = fetch(feat_in, feat, 0)
    get_weight = fetch(weight_in, weight, 1)
    get_tiles = fetch(tiles_in, tiles, 2)
    get_grad = fetch(grad_in, out_grad, 3)
    get_feat.wait()
    for hf in range(HALVES):
        for t in range(row_tiles):
            stk[hf][t] = feat[hf * hl : (hf + 1) * hl, t * tile : (t + 1) * tile]
    pl.semaphore_wait(barrier, len(peers))

    def span_of(level, k):
        return pl.ds(level * row_tiles + k * piece, piece)

    def start_features(hf):
        first = [
            send(stk[hf].at[span_of(0, k)], stk[hf].at[span_of(3, k)], me_f, me_v ^ 4)
            for k in range(CHUNKS)
        ]
        direct = [
            send(
                stk[hf].at[pl.ds(0, row_tiles)],
                stk[hf].at[pl.ds((bit + 1) * row_tiles, row_tiles)],
                me_f,
                me_v ^ (1 << bit),
            )
            for bit in (1, 0)
        ]
        return first, direct

    def hand_on(hf, first):
        handed = []
        for k, copy in enumerate(first):
            copy.wait()
            handed.append(send(stk[hf].at[span_of(3, k)], stk[hf].at[span_of(4, k)], me_f, me_v ^ 12))
        return handed

    def chain(out, picked, use_nt, prev):
        def some(g, carry):
            products = []
            for u in range(GROUP):
                c = g * GROUP + u
                if use_nt:
                    products.append(
                        lax.dot_general(picked(c), tiles[0, c], NT, preferred_element_type=F32)
                    )
                else:
                    products.append(jnp.dot(picked(c), tiles[0, c], preferred_element_type=F32))
            for u in range(GROUP):
                c = g * GROUP + u
                out[c] = products[u] + out[idx[prev, c]]
            return carry

        lax.fori_loop(0, slots // GROUP, some, 0)

    def aggregate(hf):
        chain(acc.at[hf], lambda c: stk[hf][idx[SRC, c]], True, PREV_F)
        for r in range(row_tiles):
            k = r % per
            agg[hf, r // per, :, k * tile : (k + 1) * tile] = acc[hf, idx[LAST_F, r]].astype(BF16)
        full[hf, me_f] = agg[hf, me_f]
        return [
            send(agg.at[hf, me_f ^ d], full.at[hf, me_f], me_f ^ d, me_v) for d in range(1, nf)
        ]

    first, direct = start_features(0)
    index_table(slots, row_tiles, rows_in[...], cols_in[...], counts[0], table)
    get_index = fetch(table, idx, 4)
    for hf in range(HALVES):
        acc[hf, slots] = jnp.zeros(acc.shape[2:], F32)
    get_weight.wait()
    for hf in range(HALVES):
        mine = weight[...].reshape(nf, HALVES, hl, f_all)[:, hf].reshape(f_all // HALVES, f_all)
        wt[hf] = mine.astype(F32).T.astype(BF16)
    get_index.wait()
    get_tiles.wait()
    get_grad.wait()
    moves = []
    for hf in range(HALVES):
        handed = hand_on(hf, first)
        arrivals = direct + handed
        if hf + 1 < HALVES:
            first, direct = start_features(hf + 1)
        for copy in arrivals:
            copy.wait()
        moves.append(aggregate(hf))

    blocks = 2
    block = f_all // blocks
    for hf in range(HALVES):
        for copy in moves[hf]:
            copy.wait()
    rows = [full[hf].reshape(f_all // HALVES, share) for hf in range(HALVES)]
    for i in range(blocks):
        at = slice(i * block, (i + 1) * block)
        pre = jnp.dot(wt[0, at, :], rows[0], preferred_element_type=F32)
        for hf in range(1, HALVES):
            pre = pre + jnp.dot(wt[hf, at, :], rows[hf], preferred_element_type=F32)
        sigma = jax.nn.sigmoid(pre)
        act[at, :] = (pre * sigma).astype(BF16)
        pg[at, :] = (
            out_grad[at, :].astype(F32) * sigma * (1.0 + pre * (1.0 - sigma))
        ).astype(BF16)
    grads = pg[...]
    mine = pl.ds(me_f * per, per)
    back = []
    for hf in range(HALVES):
        own = weight[...].reshape(nf, HALVES, hl, f_all)[:, hf].reshape(f_all // HALVES, f_all)
        agg_grad = jnp.dot(own, grads, preferred_element_type=F32).astype(BF16)
        for k in range(per):
            ag[hf, :, k] = agg_grad[:, k * tile : (k + 1) * tile].reshape(nf, hl, tile)
        back.append(
            [send(ag.at[hf, me_f ^ d], gc[hf].at[mine], me_f ^ d, me_v) for d in range(1, nf)]
        )
        gc[hf][mine] = ag[hf, me_f]
    for hf in range(HALVES):
        term = lax.dot_general(rows[hf], grads, NT, preferred_element_type=F32).astype(BF16)
        wgs[:, hf * hl : (hf + 1) * hl, :] = term.reshape(nf, hl, f_all)
    slab = fl // ny
    me_p = me_f * ny + y
    terms = [
        send(
            wgs.at[me_f ^ df, pl.ds((y ^ dy) * slab, slab)],
            frs.at[me_p],
            me_f ^ df,
            (y ^ dy) * NZ + z,
        )
        for df, dy in plane
    ]
    frs[me_p] = wgs[me_f, pl.ds(y * slab, slab)]

    def summed(hf, level, t):
        return acc[hf, idx[LAST_B, level * row_tiles + t]]

    direct, relayed, merged, last, steps = [], [], [], [], {}
    hr, hc = slab // 4, f_all // 4
    parts = [
        (slice(q // 4 * hr, (q // 4 + 1) * hr), slice(q % 4 * hc, (q % 4 + 1) * hc))
        for q in range(NZ)
    ]
    same_core = [(df, dy) for df, dy in plane if df % 2 == 0]

    def products(hf):
        for copy in back[hf]:
            copy.wait()
        chain(acc.at[hf], lambda c: gc[hf][idx[ROW, c]], False, PREV_B)

    def far(hf):
        for k in range(BACK):
            for t in range(k * bpiece, (k + 1) * bpiece):
                part[hf, 2, t] = summed(hf, 4, t).astype(BF16)
            span = pl.ds(k * bpiece, bpiece)
            relayed.append(send(part.at[hf, 2, span], rly.at[hf, span], me_f, me_v ^ 12))

    def near(hf):
        for bit in (1, 0):
            for t in range(row_tiles):
                part[hf, bit, t] = summed(hf, bit + 1, t).astype(BF16)
            direct.append(send(part.at[hf, bit], rv.at[hf, bit], me_f, me_v ^ (1 << bit)))

    def relay(count):
        for n in range(len(merged), len(merged) + count):
            hf, k = divmod(n, BACK)
            relayed[n].wait()
            for t in range(k * bpiece, (k + 1) * bpiece):
                mrg[hf, t] = (summed(hf, 3, t) + rly[hf, t].astype(F32)).astype(BF16)
            span = pl.ds(k * bpiece, bpiece)
            merged.append(send(mrg.at[hf, span], rv.at[hf, 2, span], me_f, me_v ^ 4))

    def scatter():
        for copy in terms:
            copy.wait()
        total = frs[0].astype(F32)
        for p in range(1, nf * ny):
            total = total + frs[p].astype(F32)
        for q, (at_r, at_c) in enumerate(parts):
            zs[q] = total[at_r, at_c]
        zr[z] = zs[z]
        steps["z"] = [send(zs.at[z ^ d], zr.at[z], me_f, me_v ^ d) for d in range(NZ - 1, 0, -1)]

    def gather():
        for copy in steps["z"]:
            copy.wait()
        total = zr[0]
        for q in range(1, NZ):
            total = total + zr[q]
        zag[z] = total
        steps["z"] = [send(zag.at[z], zag.at[z], me_f, me_v ^ d) for d in range(NZ - 1, 0, -1)]

    def spread():
        for copy in steps["z"]:
            copy.wait()
        for q, (at_r, at_c) in enumerate(parts):
            total_of[at_r, at_c] = zag[q]
        pag[me_p] = total_of[...].astype(BF16)
        steps["p"] = [
            send(pag.at[me_p], pag.at[me_p], me_f ^ df, (y ^ dy) * NZ + z) for df, dy in same_core
        ]
        last.append(send(pag.at[me_p], pag.at[me_p], me_f ^ 1, me_v))

    def pass_over():
        for (df, dy), copy in zip(same_core, steps["p"]):
            copy.wait()
            other = (me_f ^ df) * ny + (y ^ dy)
            last.append(send(pag.at[other], pag.at[other], me_f ^ 1, me_v))

    for name, *args in ORDER:
        {
            "products": products, "far": far, "near": near, "relay": relay, "scatter": scatter,
            "gather": gather, "spread": spread, "pass": pass_over,
        }[name](*args)
    for copy in direct + merged:
        copy.wait()
    for hf in range(HALVES):
        for t in range(row_tiles):
            sums = summed(hf, 0, t)
            for bit in range(3):
                sums = sums + rv[hf, bit, t].astype(F32)
            fgrad[hf * hl : (hf + 1) * hl, t * tile : (t + 1) * tile] = sums.astype(BF16)
    for copy in last:
        copy.wait()
    wgrad[...] = pag[...]


def results_kernel(act, wgrad, fgrad, act_out, wgrad_out, fgrad_out):
    act_out[...] = act[...]
    wgrad_out[...] = wgrad[...].reshape(wgrad_out.shape).astype(F32)
    fgrad_out[...] = fgrad[...]


def body(features, tiles, tile_rows, tile_cols, tile_counts, weight, output_gradient):
    fl, vdev = features.shape
    slots, tile = tiles.shape[1], tiles.shape[2]
    row_tiles = vdev // tile
    nf, nv = lax.axis_size("feat"), lax.axis_size("vert")
    ny = nv // NZ
    f_all, share = output_gradient.shape
    smem = pl.BlockSpec(memory_space=pltpu.SMEM)
    vmem = pl.BlockSpec(memory_space=pltpu.VMEM)
    hbm = pl.BlockSpec(memory_space=pltpu.HBM)
    slab = fl // ny
    hl = fl // HALVES
    copies = HALVES * (4 + 2 * CHUNKS + 2 * BACK + 2 * (nf - 1))
    copies += (nf * ny - 1) + 2 * (NZ - 1) + (nf // 2 * ny - 1) + nf // 2 * ny
    scratch = [
        (8, LANES, I32),
        (fl, vdev, BF16),
        (1, slots, tile, tile, BF16),
        (f_all, f_all, BF16),
        (f_all, share, BF16),
        ((LEVELS + 1) * row_tiles, hl, tile, BF16),
        ((LEVELS + 1) * row_tiles, hl, tile, BF16),
        (HALVES, slots + 1, hl, tile, F32),
        (HALVES, f_all, f_all // HALVES, BF16),
        (HALVES, nf, hl, share, BF16),
        (HALVES, nf, hl, share, BF16),
        (f_all, share, BF16),
        (HALVES, nf, row_tiles // nf, hl, tile, BF16),
        (row_tiles, hl, tile, BF16),
        (row_tiles, hl, tile, BF16),
        (nf, fl, f_all, BF16),
        (nf * ny, slab, f_all, BF16),
        (NZ, slab // 4, f_all // 4, F32),
        (NZ, slab // 4, f_all // 4, F32),
        (NZ, slab // 4, f_all // 4, F32),
        (slab, f_all, F32),
        (nf * ny, slab, f_all, BF16),
        (HALVES, 3, row_tiles, hl, tile, BF16),
        (HALVES, row_tiles, hl, tile, BF16),
        (HALVES, row_tiles, hl, tile, BF16),
        (HALVES, 3, row_tiles, hl, tile, BF16),
    ]
    act, wgrad, fgrad = pl.pallas_call(
        functools.partial(layer_kernel, nf, ny, slots, row_tiles, tile),
        out_shape=(
            jax.ShapeDtypeStruct((f_all, share), BF16),
            jax.ShapeDtypeStruct((nf * ny, slab, f_all), BF16),
            jax.ShapeDtypeStruct((fl, vdev), BF16),
        ),
        in_specs=[smem, vmem, vmem] + [hbm] * 4,
        out_specs=(vmem, vmem, vmem),
        scratch_shapes=[pltpu.VMEM(s[:-1], s[-1]) for s in scratch]
        + [
            pltpu.SMEM((8, LANES), I32),
            pltpu.SemaphoreType.DMA((5,)),
            pltpu.SemaphoreType.DMA((copies,)),
            pltpu.SemaphoreType.DMA((copies,)),
        ],
        compiler_params=pltpu.CompilerParams(
            collective_id=0, has_side_effects=True, vmem_limit_bytes=58 * 1024 * 1024
        ),
    )(tile_counts, tile_rows, tile_cols, features, tiles, weight, output_gradient)
    return pl.pallas_call(
        results_kernel,
        out_shape=(
            jax.ShapeDtypeStruct(act.shape, BF16),
            jax.ShapeDtypeStruct((f_all, f_all), F32),
            jax.ShapeDtypeStruct(fgrad.shape, BF16),
        ),
        in_specs=[vmem] * 3,
        out_specs=(vmem,) * 3,
    )(act, wgrad, fgrad)


def solution(mesh):
    in_specs = (
        P("feat", "vert"),
        P("vert", None, None, None),
        P("vert", None),
        P("vert", None),
        P("vert"),
        P(),
        P(None, ("vert", "feat")),
    )
    out_specs = (P(None, ("vert", "feat")), P(), P("feat", "vert"))
    return jax.shard_map(body, mesh=mesh, in_specs=in_specs, out_specs=out_specs, check_vma=False)
```

```python
import functools

import jax
import jax.numpy as jnp
from jax import lax
from jax.experimental import pallas as pl
from jax.experimental.pallas import tpu as pltpu
from jax.sharding import PartitionSpec as P

NZ = 16
LEVELS = 4
HALVES = 2
CHUNKS = 4
ORDER = (
    ("products", 0),
    ("near", 0),
    ("products", 1),
    ("scatter",),
    ("far", 0),
    ("near", 1),
    ("relay", 2),
    ("gather",),
    ("far", 1),
    ("relay", 4),
    ("spread",),
    ("relay", 2),
    ("pass",),
)
BACK = 4
GROUP = 8
SRC, ROW, PREV_F, PREV_B, LAST_F, LAST_B = range(6)
LANES = 128
MESH = pl.DeviceIdType.MESH
BF16, F32, I32 = jnp.bfloat16, jnp.float32, jnp.int32
NT = (((1,), (1,)), ((), ()))


def index_table(slots, row_tiles, rows, cols, count, table):
    across = lax.broadcasted_iota(I32, (slots, slots), 1)
    down = lax.broadcasted_iota(I32, (slots, slots), 0)
    wide = lax.broadcasted_iota(I32, (slots, LANES), 1)
    deep = lax.broadcasted_iota(I32, (slots, LANES), 0)
    valid = lax.broadcasted_iota(I32, (1, slots), 1) < count
    shift = row_tiles.bit_length() - 1
    differ = lax.shift_right_arithmetic(cols, shift) ^ lax.axis_index("vert")
    level = jnp.zeros(cols.shape, I32)
    for bit in range(LEVELS):
        level = level + jnp.where(differ >= (1 << bit), 1, 0).astype(I32)
    target = jnp.where(valid, level * row_tiles + (cols & (row_tiles - 1)), 0)
    line = jnp.where(valid, rows, 0)
    table[SRC : SRC + 1, :slots] = target
    table[ROW : ROW + 1, :slots] = line
    for key, prev_at, last_at in ((line, PREV_F, LAST_F), (target, PREV_B, LAST_B)):
        key = jnp.where(valid, key, -1)
        column = jnp.max(jnp.where(across == down, key, -1), axis=1, keepdims=True)
        same = (column == key) & (down < across) & (column >= 0)
        before = jnp.max(jnp.where(same, down, -1), axis=0, keepdims=True)
        table[prev_at : prev_at + 1, :slots] = jnp.where(before < 0, slots, before)
        final = jnp.max(jnp.where(column == wide, deep, -1), axis=0, keepdims=True)
        table[last_at : last_at + 1, :] = jnp.where(final < 0, slots, final)


def layer_kernel(
    nf, ny, slots, row_tiles, tile,
    counts, rows_in, cols_in, feat_in, tiles_in, weight_in, grad_in,
    act, wgrad, fgrad,
    table, feat, tiles, weight, out_grad,
    stk0, stk1, acc, wt, agg, full, pg, ag, gc0, gc1, wgs, frs, zs, zr, zag, total_of, pag,
    part, rly, mrg, rv, idx, lsem, ssem, rsem,
):
    stk, gc = (stk0, stk1), (gc0, gc1)
    fl = feat.shape[0]
    f_all = nf * fl
    hl = fl // HALVES
    per = row_tiles // nf
    share = per * tile
    me_f, me_v = lax.axis_index("feat"), lax.axis_index("vert")
    z, y = me_v % NZ, me_v // NZ
    piece, bpiece = row_tiles // CHUNKS, row_tiles // BACK

    used = [0]

    def send(source, dest, f, v):
        n = used[0]
        used[0] += 1
        copy = pltpu.make_async_remote_copy(
            source, dest, ssem.at[n], rsem.at[n], device_id=(f, v), device_id_type=MESH
        )
        copy.start()
        return copy

    def fetch(source, dest, n):
        copy = pltpu.make_async_copy(source, dest, lsem.at[n])
        copy.start()
        return copy

    peers = [(me_f, me_v ^ d) for d in range(NZ - 1, 0, -1)]
    plane = [(df, dy) for df in range(nf) for dy in range(ny) if df or dy]
    peers += [(me_f ^ df, (y ^ dy) * NZ + z) for df, dy in plane]
    barrier = pltpu.get_barrier_semaphore()
    for f, v in peers:
        pl.semaphore_signal(barrier, inc=1, device_id=(f, v), device_id_type=MESH)
    get_feat = fetch(feat_in, feat, 0)
    get_weight = fetch(weight_in, weight, 1)
    get_tiles = fetch(tiles_in, tiles, 2)
    get_grad = fetch(grad_in, out_grad, 3)
    get_feat.wait()
    for hf in range(HALVES):
        for t in range(row_tiles):
            stk[hf][t] = feat[hf * hl : (hf + 1) * hl, t * tile : (t + 1) * tile]
    pl.semaphore_wait(barrier, len(peers))

    def span_of(level, k):
        return pl.ds(level * row_tiles + k * piece, piece)

    def start_features(hf):
        first = [
            send(stk[hf].at[span_of(0, k)], stk[hf].at[span_of(3, k)], me_f, me_v ^ 4)
            for k in range(CHUNKS)
        ]
        direct = [
            send(
                stk[hf].at[pl.ds(0, row_tiles)],
                stk[hf].at[pl.ds((bit + 1) * row_tiles, row_tiles)],
                me_f,
                me_v ^ (1 << bit),
            )
            for bit in (1, 0)
        ]
        return first, direct

    def hand_on(hf, first):
        handed = []
        for k, copy in enumerate(first):
            copy.wait()
            handed.append(send(stk[hf].at[span_of(3, k)], stk[hf].at[span_of(4, k)], me_f, me_v ^ 12))
        return handed

    def chain(out, picked, use_nt, prev):
        def some(g, carry):
            products = []
            for u in range(GROUP):
                c = g * GROUP + u
                if use_nt:
                    products.append(
                        lax.dot_general(picked(c), tiles[0, c], NT, preferred_element_type=F32)
                    )
                else:
                    products.append(jnp.dot(picked(c), tiles[0, c], preferred_element_type=F32))
            for u in range(GROUP):
                c = g * GROUP + u
                out[c] = products[u] + out[idx[prev, c]]
            return carry

        lax.fori_loop(0, slots // GROUP, some, 0)

    def aggregate(hf):
        chain(acc.at[hf], lambda c: stk[hf][idx[SRC, c]], True, PREV_F)
        for r in range(row_tiles):
            k = r % per
            agg[hf, r // per, :, k * tile : (k + 1) * tile] = acc[hf, idx[LAST_F, r]].astype(BF16)
        full[hf, me_f] = agg[hf, me_f]
        return [
            send(agg.at[hf, me_f ^ d], full.at[hf, me_f], me_f ^ d, me_v) for d in range(1, nf)
        ]

    first, direct = start_features(0)
    index_table(slots, row_tiles, rows_in[...], cols_in[...], counts[0], table)
    get_index = fetch(table, idx, 4)
    for hf in range(HALVES):
        acc[hf, slots] = jnp.zeros(acc.shape[2:], F32)
    get_weight.wait()
    for hf in range(HALVES):
        mine = weight[...].reshape(nf, HALVES, hl, f_all)[:, hf].reshape(f_all // HALVES, f_all)
        wt[hf] = mine.astype(F32).T.astype(BF16)
    get_index.wait()
    get_tiles.wait()
    get_grad.wait()
    moves = []
    for hf in range(HALVES):
        handed = hand_on(hf, first)
        arrivals = direct + handed
        if hf + 1 < HALVES:
            first, direct = start_features(hf + 1)
        for copy in arrivals:
            copy.wait()
        moves.append(aggregate(hf))

    blocks = 2
    block = f_all // blocks
    for hf in range(HALVES):
        for copy in moves[hf]:
            copy.wait()
    rows = [full[hf].reshape(f_all // HALVES, share) for hf in range(HALVES)]
    for i in range(blocks):
        at = slice(i * block, (i + 1) * block)
        pre = jnp.dot(wt[0, at, :], rows[0], preferred_element_type=F32)
        for hf in range(1, HALVES):
            pre = pre + jnp.dot(wt[hf, at, :], rows[hf], preferred_element_type=F32)
        sigma = jax.nn.sigmoid(pre)
        act[at, :] = (pre * sigma).astype(BF16)
        pg[at, :] = (
            out_grad[at, :].astype(F32) * sigma * (1.0 + pre * (1.0 - sigma))
        ).astype(BF16)
    grads = pg[...]
    mine = pl.ds(me_f * per, per)
    back = []
    def give_back(hf):
        own = weight[...].reshape(nf, HALVES, hl, f_all)[:, hf].reshape(f_all // HALVES, f_all)
        agg_grad = jnp.dot(own, grads, preferred_element_type=F32).astype(BF16)
        for k in range(per):
            ag[hf, :, k] = agg_grad[:, k * tile : (k + 1) * tile].reshape(nf, hl, tile)
        back.append(
            [send(ag.at[hf, me_f ^ d], gc[hf].at[mine], me_f ^ d, me_v) for d in range(1, nf)]
        )
        gc[hf][mine] = ag[hf, me_f]

    give_back(0)
    for hf in range(HALVES):
        term = lax.dot_general(rows[hf], grads, NT, preferred_element_type=F32).astype(BF16)
        wgs[:, hf * hl : (hf + 1) * hl, :] = term.reshape(nf, hl, f_all)
    slab = fl // ny
    me_p = me_f * ny + y
    terms = [
        send(
            wgs.at[me_f ^ df, pl.ds((y ^ dy) * slab, slab)],
            frs.at[me_p],
            me_f ^ df,
            (y ^ dy) * NZ + z,
        )
        for df, dy in plane
    ]
    frs[me_p] = wgs[me_f, pl.ds(y * slab, slab)]
    for hf in range(1, HALVES):
        give_back(hf)

    def summed(hf, level, t):
        return acc[hf, idx[LAST_B, level * row_tiles + t]]

    direct, relayed, merged, last, steps = [], [], [], [], {}
    hr, hc = slab // 4, f_all // 4
    parts = [
        (slice(q // 4 * hr, (q // 4 + 1) * hr), slice(q % 4 * hc, (q % 4 + 1) * hc))
        for q in range(NZ)
    ]
    same_core = [(df, dy) for df, dy in plane if df % 2 == 0]

    def products(hf):
        for copy in back[hf]:
            copy.wait()
        chain(acc.at[hf], lambda c: gc[hf][idx[ROW, c]], False, PREV_B)

    def far(hf):
        for k in range(BACK):
            for t in range(k * bpiece, (k + 1) * bpiece):
                part[hf, 2, t] = summed(hf, 4, t).astype(BF16)
            span = pl.ds(k * bpiece, bpiece)
            relayed.append(send(part.at[hf, 2, span], rly.at[hf, span], me_f, me_v ^ 12))

    def near(hf):
        for bit in (1, 0):
            for t in range(row_tiles):
                part[hf, bit, t] = summed(hf, bit + 1, t).astype(BF16)
            direct.append(send(part.at[hf, bit], rv.at[hf, bit], me_f, me_v ^ (1 << bit)))

    def relay(count):
        for n in range(len(merged), len(merged) + count):
            hf, k = divmod(n, BACK)
            relayed[n].wait()
            for t in range(k * bpiece, (k + 1) * bpiece):
                mrg[hf, t] = (summed(hf, 3, t) + rly[hf, t].astype(F32)).astype(BF16)
            span = pl.ds(k * bpiece, bpiece)
            merged.append(send(mrg.at[hf, span], rv.at[hf, 2, span], me_f, me_v ^ 4))

    def scatter():
        for copy in terms:
            copy.wait()
        total = frs[0].astype(F32)
        for p in range(1, nf * ny):
            total = total + frs[p].astype(F32)
        for q, (at_r, at_c) in enumerate(parts):
            zs[q] = total[at_r, at_c]
        zr[z] = zs[z]
        steps["z"] = [send(zs.at[z ^ d], zr.at[z], me_f, me_v ^ d) for d in range(NZ - 1, 0, -1)]

    def gather():
        for copy in steps["z"]:
            copy.wait()
        total = zr[0]
        for q in range(1, NZ):
            total = total + zr[q]
        zag[z] = total
        steps["z"] = [send(zag.at[z], zag.at[z], me_f, me_v ^ d) for d in range(NZ - 1, 0, -1)]

    def spread():
        for copy in steps["z"]:
            copy.wait()
        for q, (at_r, at_c) in enumerate(parts):
            total_of[at_r, at_c] = zag[q]
        pag[me_p] = total_of[...].astype(BF16)
        steps["p"] = [
            send(pag.at[me_p], pag.at[me_p], me_f ^ df, (y ^ dy) * NZ + z) for df, dy in same_core
        ]
        last.append(send(pag.at[me_p], pag.at[me_p], me_f ^ 1, me_v))

    def pass_over():
        for (df, dy), copy in zip(same_core, steps["p"]):
            copy.wait()
            other = (me_f ^ df) * ny + (y ^ dy)
            last.append(send(pag.at[other], pag.at[other], me_f ^ 1, me_v))

    for name, *args in ORDER:
        {
            "products": products, "far": far, "near": near, "relay": relay, "scatter": scatter,
            "gather": gather, "spread": spread, "pass": pass_over,
        }[name](*args)
    for copy in direct + merged:
        copy.wait()
    for hf in range(HALVES):
        for t in range(row_tiles):
            sums = summed(hf, 0, t)
            for bit in range(3):
                sums = sums + rv[hf, bit, t].astype(F32)
            fgrad[hf * hl : (hf + 1) * hl, t * tile : (t + 1) * tile] = sums.astype(BF16)
    for copy in last:
        copy.wait()
    wgrad[...] = pag[...]


def results_kernel(act, wgrad, fgrad, act_out, wgrad_out, fgrad_out):
    act_out[...] = act[...]
    wgrad_out[...] = wgrad[...].reshape(wgrad_out.shape).astype(F32)
    fgrad_out[...] = fgrad[...]


def body(features, tiles, tile_rows, tile_cols, tile_counts, weight, output_gradient):
    fl, vdev = features.shape
    slots, tile = tiles.shape[1], tiles.shape[2]
    row_tiles = vdev // tile
    nf, nv = lax.axis_size("feat"), lax.axis_size("vert")
    ny = nv // NZ
    f_all, share = output_gradient.shape
    smem = pl.BlockSpec(memory_space=pltpu.SMEM)
    vmem = pl.BlockSpec(memory_space=pltpu.VMEM)
    hbm = pl.BlockSpec(memory_space=pltpu.HBM)
    slab = fl // ny
    hl = fl // HALVES
    copies = HALVES * (4 + 2 * CHUNKS + 2 * BACK + 2 * (nf - 1))
    copies += (nf * ny - 1) + 2 * (NZ - 1) + (nf // 2 * ny - 1) + nf // 2 * ny
    scratch = [
        (8, LANES, I32),
        (fl, vdev, BF16),
        (1, slots, tile, tile, BF16),
        (f_all, f_all, BF16),
        (f_all, share, BF16),
        ((LEVELS + 1) * row_tiles, hl, tile, BF16),
        ((LEVELS + 1) * row_tiles, hl, tile, BF16),
        (HALVES, slots + 1, hl, tile, F32),
        (HALVES, f_all, f_all // HALVES, BF16),
        (HALVES, nf, hl, share, BF16),
        (HALVES, nf, hl, share, BF16),
        (f_all, share, BF16),
        (HALVES, nf, row_tiles // nf, hl, tile, BF16),
        (row_tiles, hl, tile, BF16),
        (row_tiles, hl, tile, BF16),
        (nf, fl, f_all, BF16),
        (nf * ny, slab, f_all, BF16),
        (NZ, slab // 4, f_all // 4, F32),
        (NZ, slab // 4, f_all // 4, F32),
        (NZ, slab // 4, f_all // 4, F32),
        (slab, f_all, F32),
        (nf * ny, slab, f_all, BF16),
        (HALVES, 3, row_tiles, hl, tile, BF16),
        (HALVES, row_tiles, hl, tile, BF16),
        (HALVES, row_tiles, hl, tile, BF16),
        (HALVES, 3, row_tiles, hl, tile, BF16),
    ]
    act, wgrad, fgrad = pl.pallas_call(
        functools.partial(layer_kernel, nf, ny, slots, row_tiles, tile),
        out_shape=(
            jax.ShapeDtypeStruct((f_all, share), BF16),
            jax.ShapeDtypeStruct((nf * ny, slab, f_all), BF16),
            jax.ShapeDtypeStruct((fl, vdev), BF16),
        ),
        in_specs=[smem, vmem, vmem] + [hbm] * 4,
        out_specs=(vmem, vmem, vmem),
        scratch_shapes=[pltpu.VMEM(s[:-1], s[-1]) for s in scratch]
        + [
            pltpu.SMEM((8, LANES), I32),
            pltpu.SemaphoreType.DMA((5,)),
            pltpu.SemaphoreType.DMA((copies,)),
            pltpu.SemaphoreType.DMA((copies,)),
        ],
        compiler_params=pltpu.CompilerParams(
            collective_id=0, has_side_effects=True, vmem_limit_bytes=58 * 1024 * 1024
        ),
    )(tile_counts, tile_rows, tile_cols, features, tiles, weight, output_gradient)
    return pl.pallas_call(
        results_kernel,
        out_shape=(
            jax.ShapeDtypeStruct(act.shape, BF16),
            jax.ShapeDtypeStruct((f_all, f_all), F32),
            jax.ShapeDtypeStruct(fgrad.shape, BF16),
        ),
        in_specs=[vmem] * 3,
        out_specs=(vmem,) * 3,
    )(act, wgrad, fgrad)


def solution(mesh):
    in_specs = (
        P("feat", "vert"),
        P("vert", None, None, None),
        P("vert", None),
        P("vert", None),
        P("vert"),
        P(),
        P(None, ("vert", "feat")),
    )
    out_specs = (P(None, ("vert", "feat")), P(), P("feat", "vert"))
    return jax.shard_map(body, mesh=mesh, in_specs=in_specs, out_specs=out_specs, check_vma=False)
```
